32 devices in a mesh: band: 16 (over z, x, core), mem: 2 (over y).
Axes of the slice: x: 2, y: 2, z: 4, core: 2. Of those that a mesh axis runs over, the one named last changes fastest.
Arguments:
- spectra: bfloat16 [4, 4, 2, 2, 901120], P('mem', None, None, None, 'band'), may hold values from -6 to 6
- legendre: bfloat16 [10, 901120], P(None, 'band'), may hold values from -0.0034179688 to 0.0034179688
- pair_waves: int32 [640], P('band'), may hold values from 0 to 639, each once
- band_lengths: int32 [16], replicated, may hold values from 1 to 2, 20 in all
- eof_basis: bfloat16 [32, 2560, 256], P('band'), may hold values from -0.0390625 to 0.0390625
Outputs:
- grid_fields: bfloat16 [4, 4, 2, 32, 2560], P('mem', None, None, 'band')
- eof_coeffs: float32 [4, 4, 2, 256], P('mem', None, None, 'band')
The draws below stay inside these ranges and needn't reach their ends.
Inputs may be any that keep to these rules, and one draw needn't show every extreme that they name: `pair_waves`: every lower wavenumber 0 .. 639 stands in exactly one pair slot. `band_lengths`: the lengths sum to 20; some band has exactly 2 rows.
All inputs are finite; a program needn't handle non-finite values.
Results may differ from the reference program's by a relative error of at most 0.0055.
Values may be sent and summed in bfloat16 or wider, within the bound.
A program may use at most 192 MiB of HBM per device.

```python
import math
from functools import partial
import jax
import jax.numpy as jnp
import numpy as np
from jax import lax

WAVE_COUNT = 1280
LON = 2560
NEOF = 256
FIELD_COUNT = 4
LEVEL_COUNT = 2
LMAX = 2
BLK = 128
MEMBER_COUNT = 4
BANDS = 16
LAT = 20
HALF_LATITUDES = 10
PAIR_LEN = 1408
SLOT_TOTAL = 901120
LSLOTS = 32


def raised(entries, own_key, source, target, parts, factor):
    def block_of(axis_at):
        return (jnp.arange(entries.shape[axis_at]) // (entries.shape[axis_at] // parts)).reshape((-1,) + (1,) * (entries.ndim - 1 - axis_at))

    one_side = jax.random.permutation(own_key, parts)[block_of(target)]
    far = (block_of(target) + parts // 2) % parts
    return jnp.where((block_of(source) == one_side) | (block_of(source) == far), factor * entries, entries)


def level_of(rng, shape, shards, least, largest):
    factor_of, own = 1.0, jax.random.fold_in(rng, 6)
    for axis_at, parts in shards:
        heights = jnp.exp(jax.random.uniform(jax.random.fold_in(own, axis_at), (parts,), jnp.float32, least / len(shards), largest / len(shards)))
        factor_of = factor_of * jnp.repeat(heights, shape[axis_at] // parts).reshape([-1 if axis == axis_at else 1 for axis in range(len(shape))])
    return factor_of


def split_up(amount, total, bound, slope):
    weights = [(1 << 20) // math.isqrt(grade ** slope) + 1 for grade in range(2, amount + 1)]
    surplus, holding = total - bound - (amount - 1), [1] * (amount - 1)
    while surplus > 0:
        free = [i for i in range(amount - 1) if holding[i] < bound]
        whole, remaining = sum([weights[i] for i in free]), surplus
        for i in free:
            extra = min(bound - holding[i], max(1, remaining * weights[i] // whole), surplus)
            holding[i] = holding[i] + extra
            surplus = surplus - extra
    return np.array([bound] + holding)


def ragged(rng, amount, total, most, lean):
    if amount == 2:
        one = jax.random.randint(rng, (), max(1, total - most), min(most, total - 1) + 1)
        return jnp.stack([one, total - one])
    tallies = jnp.asarray(split_up(amount, total, most, lean), jnp.int32)
    twos = (amount - 1) // 2
    donor, sink = tallies[1:1 + 2 * twos:2], tallies[2:2 + 2 * twos:2]
    room = jnp.minimum(donor - 1, most - sink)
    passed = jax.random.randint(jax.random.fold_in(rng, 1), (twos,), 0, 1 << 20) % (room + 1)
    tallies = tallies.at[1:1 + 2 * twos:2].set(donor - passed).at[2:2 + 2 * twos:2].set(sink + passed)
    return tallies[jax.random.permutation(jax.random.fold_in(rng, 2), amount)]


def scatter_about(stream_key, dims, width, bound, split=(), held_as=jnp.bfloat16):
    values = width * jax.random.normal(stream_key, dims, jnp.float32)
    if split:
        values = values * level_of(stream_key, dims, split, -0.22, 0.18)
    return jnp.clip(values, -bound, bound).astype(held_as)


def heavy_noise(key, shape, width, bound, split, heavy, kind=jnp.bfloat16):
    entries = width * jax.random.normal(key, shape, jnp.float32)
    if split:
        entries = entries * level_of(key, shape, split, -0.22, 0.18)
    return jnp.clip(raised(entries, jax.random.fold_in(key, 3), *heavy), -bound, bound).astype(kind)


def setup_inputs(seed: int = 0) -> dict:
    seeds = jax.random.split(jax.random.key(seed), 6)
    spectra = scatter_about(seeds[0], (MEMBER_COUNT, FIELD_COUNT, LEVEL_COUNT, 2, SLOT_TOTAL), 1.0, 6.0, ((0, 2), (4, 16)))
    legendre = scatter_about(seeds[1], (HALF_LATITUDES, SLOT_TOTAL), (2 * WAVE_COUNT * WAVE_COUNT) ** -0.5, 0.0034179688, ((1, 16),))
    pair_waves = jax.random.permutation(seeds[2], WAVE_COUNT // 2).astype(jnp.int32)
    band_lengths = ragged(seeds[3], BANDS, LAT, LMAX, 2).astype(jnp.int32)
    eof_basis = heavy_noise(seeds[4], (LSLOTS, LON, NEOF), (LAT * LON) ** -0.5, 0.0390625, ((0, 16),), (0, 2, 16, 2.0))
    return dict(spectra=spectra, legendre=legendre, pair_waves=pair_waves, band_lengths=band_lengths, eof_basis=eof_basis)


def wave_table(orders, length):
    lon_index = jnp.arange(length, dtype=jnp.int32)
    phase_idx = (orders[..., None] * lon_index) % length
    angle_rad = phase_idx.astype(jnp.float32) * (2.0 * math.pi / length)
    weight = jnp.where(orders == 0, 1.0, 2.0).astype(jnp.float32)[..., None]
    return jnp.stack([weight * jnp.cos(angle_rad), -weight * jnp.sin(angle_rad)]).astype(jnp.bfloat16)


def pair_fourier(flat_spectral_coeffs, legendre, pair_waves, pair_slot):
    slot_start = (pair_slot * PAIR_LEN).astype(jnp.int32)
    coeffs = lax.dynamic_slice_in_dim(flat_spectral_coeffs, slot_start, PAIR_LEN, 1).astype(jnp.float32)
    rows_tab = lax.dynamic_slice_in_dim(legendre, slot_start, PAIR_LEN, 1).astype(jnp.float32)
    lower_wave = pair_waves[pair_slot]
    position = jnp.arange(PAIR_LEN, dtype=jnp.int32)
    low_blocks = WAVE_COUNT // BLK - lower_wave // BLK
    upper_pos = position - low_blocks * BLK
    low_mask = (position < WAVE_COUNT - lower_wave).astype(jnp.float32)
    high_mask = ((upper_pos >= 0) & (upper_pos < lower_wave + 1)).astype(jnp.float32)
    alternate = jnp.where(position % 2 == 0, 1.0, -1.0).astype(jnp.float32)
    south_tab = rows_tab * alternate
    outputs = []
    for mask_row in (low_mask, high_mask):
        masked = coeffs * mask_row
        north_part = jnp.dot(masked, rows_tab.T, precision=lax.Precision.HIGHEST)
        south_part = jnp.dot(masked, south_tab.T, precision=lax.Precision.HIGHEST)
        outputs.append(jnp.concatenate([north_part, south_part[:, ::-1]], axis=1))
    return jnp.stack(outputs)


def reference(spectra, legendre, pair_waves, band_lengths, eof_basis):
    flat_spectral_coeffs = spectra.reshape(MEMBER_COUNT * FIELD_COUNT * LEVEL_COUNT * 2, SLOT_TOTAL)
    fourier = lax.map(partial(pair_fourier, flat_spectral_coeffs, legendre, pair_waves), jnp.arange(WAVE_COUNT // 2, dtype=jnp.int32))
    fourier = lax.optimization_barrier(fourier.astype(jnp.bfloat16)).astype(jnp.float32)
    fourier = fourier.reshape(WAVE_COUNT // 2, 2, MEMBER_COUNT, FIELD_COUNT, LEVEL_COUNT, 2, LAT)
    orders = jnp.stack([pair_waves, WAVE_COUNT - 1 - pair_waves], axis=1)
    wave_cos = wave_table(orders, LON).astype(jnp.float32)
    grid_sum = jnp.einsum("phabdcj,cphk->abdjk", fourier, wave_cos, precision=lax.Precision.HIGHEST)
    grid_lat = grid_sum.astype(jnp.bfloat16)
    starts = (jnp.cumsum(band_lengths) - band_lengths).astype(jnp.int32)
    offsets = jnp.arange(LMAX, dtype=jnp.int32)
    row_index = jnp.minimum(starts[:, None] + offsets[None, :], LAT - 1).reshape(-1).astype(jnp.int32)
    row_keep = (offsets[None, :] < band_lengths[:, None]).reshape(-1)
    picked = jnp.take(grid_lat, row_index, axis=3)
    grid_fields = jnp.where(row_keep[:, None], picked, jnp.zeros((), picked.dtype)).astype(jnp.bfloat16)
    flat_grid = grid_fields.reshape(MEMBER_COUNT * FIELD_COUNT * LEVEL_COUNT, LSLOTS * LON)
    projection = jnp.dot(flat_grid, eof_basis.reshape(LSLOTS * LON, NEOF), preferred_element_type=jnp.float32)
    projection = projection.reshape(MEMBER_COUNT, FIELD_COUNT * LEVEL_COUNT, NEOF)
    anomaly = projection - jnp.mean(projection, axis=0, keepdims=True)
    return grid_fields, anomaly.reshape(MEMBER_COUNT, FIELD_COUNT, LEVEL_COUNT, NEOF)
```

```python
import math

import jax
import jax.numpy as jnp
import ml_dtypes
import numpy as np
from jax import lax
from jax.experimental import pallas as pl
from jax.experimental.pallas import tpu as pltpu
from jax.sharding import PartitionSpec as P

WAVE_COUNT = 1280
BLK = 128
HALF = WAVE_COUNT // 2
F32 = jnp.float32
BF16 = jnp.bfloat16
VMEM_LIMIT = 48 * 1024 * 1024


def iota(shape, axis):
    return lax.broadcasted_iota(jnp.int32, shape, axis)


def round_up(number, multiple):
    return -(-number // multiple) * multiple


def group_of(count, most):
    return max(size for size in range(1, most + 1) if count % size == 0)


def legendre_kernel(
    waves_smem, spectra_ref, legendre_ref, lengths_ref, waves_ref, out_ref, select_ref, total_ref,
    *, group, lat_half, lat_pad, bands, rows, pairs,
):
    step = pl.program_id(0)
    pair_len = legendre_ref.shape[1] // group
    fields = spectra_ref.shape[0]
    columns = 2 * fields
    width = 2 * rows * columns

    @pl.when(step == 0)
    def _():
        shape = (2 * rows * bands, 4 * lat_pad)
        slot = iota((2 * rows * bands, bands), 0)
        band = slot % bands
        lane = iota((2 * rows * bands, bands), 1)
        lengths = lengths_ref[...]
        start = jnp.sum(jnp.where(lane < band, lengths, 0).astype(F32), axis=1, keepdims=True)
        own = jnp.sum(jnp.where(lane == band, lengths, 0).astype(F32), axis=1, keepdims=True)
        slot = iota(shape, 0)
        row = slot // bands % rows
        place = iota(shape, 1)
        lat = jnp.broadcast_to(start, shape).astype(jnp.int32) + row
        keep = row < jnp.broadcast_to(own, shape).astype(jnp.int32)
        wanted = jnp.where(lat < lat_half, lat, lat_pad + 2 * lat_half - 1 - lat)
        wanted = wanted + slot // (bands * rows) * (2 * lat_pad)
        select_ref[...] = jnp.where(keep & (place == wanted), 1.0, 0.0).astype(BF16)

    widen = (iota((lat_pad, lat_half), 0) == iota((lat_pad, lat_half), 1)).astype(BF16)
    position = iota((lat_pad, pair_len), 1)
    even = position % 2 == 0
    lane_in = iota((width, width), 0)
    lane_out = iota((width, width), 1)
    block, rest = lane_in // columns, lane_in % columns
    target = ((block // rows * 2 + rest % 2) * rows + block % rows) * fields + rest // 2
    reorder = (lane_out == target).astype(BF16)
    for index in range(group):
        span = pl.ds(index * pair_len, pair_len)
        lower = waves_smem[step * group + index]
        high_start = WAVE_COUNT - lower // BLK * BLK
        low = position < WAVE_COUNT - lower
        high = (position >= high_start) & (position < high_start + lower + 1)
        table = jnp.dot(widen, legendre_ref[:, span], preferred_element_type=F32)
        weights = jnp.concatenate(
            [jnp.where(mask & parity, table, 0.0) for mask in (low, high) for parity in (even, ~even)],
            axis=0,
        ).astype(BF16)
        coeffs = spectra_ref[:, :, span].reshape(columns, pair_len)
        sums = lax.dot_general(
            weights, coeffs, (((1,), (1,)), ((), ())), preferred_element_type=F32
        )
        parts = [sums[i * lat_pad : (i + 1) * lat_pad] for i in range(4)]
        fourier = jnp.concatenate(
            [parts[0] + parts[1], parts[0] - parts[1], parts[2] + parts[3], parts[2] - parts[3]],
            axis=0,
        ).astype(BF16)
        picked = jnp.dot(select_ref[...], fourier, preferred_element_type=F32)
        wide = jnp.concatenate(
            [picked[i * bands : (i + 1) * bands] for i in range(2 * rows)], axis=1
        ).astype(BF16)
        total_ref[step * group + index] = jnp.dot(wide, reorder, preferred_element_type=F32)

    @pl.when(step == pl.num_programs(0) - 1)
    def _():
        pad = out_ref.shape[1] - pairs
        waves = waves_ref[...]
        kind = iota((pad, width), 0)
        extra = jnp.where(
            kind == 0, (waves // BLK).astype(F32), jnp.where(kind == 1, (waves % BLK).astype(F32), 0.0)
        )
        total = jnp.swapaxes(total_ref[...], 0, 1)
        extra = jnp.broadcast_to(extra[None], (bands, pad, width))
        out_ref[...] = jnp.concatenate([total, extra], axis=1).astype(BF16)


def synthesis_kernel(
    arrived_ref, table_ref, first_eof_ref, last_eof_ref, first_ref, last_ref, projection_ref,
    waves_in_ref, *, bands, rows, pairs,
):
    step = pl.program_id(0)
    taken = arrived_ref.shape[1]
    width = arrived_ref.shape[2]
    fields = width // (4 * rows)

    @pl.when(step == 0)
    def _():
        projection_ref[...] = jnp.zeros_like(projection_ref)
        count = bands * taken
        arrived = arrived_ref[...]
        coded = arrived.astype(F32)
        high = jnp.sum(jnp.where(iota(coded.shape, 1) == pairs, coded, 0.0), axis=1)
        low = jnp.sum(jnp.where(iota(coded.shape, 1) == pairs + 1, coded, 0.0), axis=1)
        waves = high * BLK + low
        waves = jnp.broadcast_to(waves[:, None, :], (bands, taken, width))
        slot = iota(waves.shape, 1)
        lane = iota(waves.shape, 2)
        own = jnp.sum(jnp.where(slot == lane, waves, 0.0), axis=2, keepdims=True)
        own = jnp.where(iota(own.shape, 1) < pairs, own, -1.0).reshape(count, 1)
        place = iota((count, HALF), 1)
        order = jnp.where(place < HALF // 2, 2 * place, 2 * place - (HALF - 1)).astype(F32)
        match = jnp.where(own == order, 1.0, 0.0).astype(BF16)
        ordered = lax.dot_general(
            arrived.reshape(count, width), match, (((0,), (0,)), ((), ())), preferred_element_type=F32
        )
        quarter = rows * fields
        first_half = iota((2 * quarter, HALF), 1) < HALF // 2
        low_order, high_order = ordered[: 2 * quarter], ordered[2 * quarter :]
        waves_in_ref[0] = jnp.where(first_half, low_order, high_order).astype(BF16)
        waves_in_ref[1] = jnp.where(first_half, high_order, low_order).astype(BF16)

    quarter = rows * fields
    even, odd = (
        jnp.dot(waves_in_ref[parity, :quarter], table_ref[parity, 0], preferred_element_type=F32)
        + jnp.dot(waves_in_ref[parity, quarter:], table_ref[parity, 1], preferred_element_type=F32)
        for parity in range(2)
    )
    total = projection_ref[...]
    for out, eof, value in ((first_ref, first_eof_ref, even + odd), (last_ref, last_eof_ref, even - odd)):
        value = value.astype(BF16)
        for row in range(rows):
            part = value[row * fields : (row + 1) * fields]
            out[row] = part
            total += jnp.dot(part, eof[row], preferred_element_type=F32)
    projection_ref[...] = total


def wave_tables(longitudes):
    place = np.arange(HALF)
    lower = np.where(place < HALF // 2, 2 * place, 2 * place - (HALF - 1))
    upper = WAVE_COUNT - 1 - lower
    even = np.where(lower % 2 == 0, lower, upper)
    orders = np.stack([even, WAVE_COUNT - 1 - even])
    phase = orders[..., None] * np.arange(longitudes // 2) % longitudes
    angle = phase * (2.0 * math.pi / longitudes)
    weight = np.where(orders == 0, 1.0, 2.0)[..., None]
    table = np.stack([weight * np.cos(angle), -weight * np.sin(angle)], axis=1)
    return table.astype(np.float32).astype(ml_dtypes.bfloat16)


def shards(spectra, legendre, pair_waves, band_lengths, eof_basis):
    members, fields, levels, re_im, slot_count = spectra.shape
    lat_half = legendre.shape[0]
    pairs = pair_waves.shape[0]
    pair_len = slot_count // pairs
    stack = members * fields * levels
    bands = lax.axis_size("band")
    rows, longitudes, modes = eof_basis.shape
    width = 2 * rows * stack * re_im
    group = group_of(pairs, 8)
    lat_pad = round_up(lat_half, 16)
    taken = round_up(pairs + 2, 16)
    wave_row = jnp.pad(pair_waves, (0, width - pairs)).reshape(1, width)

    def fixed(*shape):
        return pl.BlockSpec(shape, lambda *_: (0,) * len(shape))

    payload = pl.pallas_call(
        lambda *refs: legendre_kernel(
            *refs, group=group, lat_half=lat_half, lat_pad=lat_pad, bands=bands, rows=rows, pairs=pairs
        ),
        out_shape=jax.ShapeDtypeStruct((bands, taken, width), BF16),
        grid_spec=pltpu.PrefetchScalarGridSpec(
            num_scalar_prefetch=1,
            grid=(pairs // group,),
            in_specs=[
                pl.BlockSpec((stack, re_im, group * pair_len), lambda i, _: (0, 0, i)),
                pl.BlockSpec((lat_half, group * pair_len), lambda i, _: (0, i)),
                fixed(1, bands),
                fixed(1, width),
            ],
            out_specs=fixed(bands, taken, width),
            scratch_shapes=[
                pltpu.VMEM((2 * rows * bands, 4 * lat_pad), BF16),
                pltpu.VMEM((pairs, bands, width), F32),
            ],
        ),
        compiler_params=pltpu.CompilerParams(vmem_limit_bytes=VMEM_LIMIT),
        name="legendre",
    )(
        pair_waves,
        spectra.reshape(stack, re_im, slot_count),
        legendre,
        band_lengths.reshape(1, bands),
        wave_row,
    )
    arrived = lax.all_to_all(payload, "band", split_axis=0, concat_axis=0, tiled=True)
    lon_width = math.gcd(longitudes // 2, 256)
    steps = longitudes // 2 // lon_width
    table = jnp.asarray(wave_tables(longitudes))
    half_shape = jax.ShapeDtypeStruct((rows, stack, longitudes // 2), BF16)
    first, last, partial = pl.pallas_call(
        lambda *refs: synthesis_kernel(*refs, bands=bands, rows=rows, pairs=pairs),
        out_shape=(half_shape, half_shape, jax.ShapeDtypeStruct((stack, modes), F32)),
        grid=(steps,),
        in_specs=[
            fixed(bands, taken, width),
            pl.BlockSpec((2, 2, HALF, lon_width), lambda i: (0, 0, 0, i)),
            pl.BlockSpec((rows, lon_width, modes), lambda i: (0, i, 0)),
            pl.BlockSpec((rows, lon_width, modes), lambda i: (0, i + steps, 0)),
        ],
        out_specs=(
            pl.BlockSpec((rows, stack, lon_width), lambda i: (0, 0, i)),
            pl.BlockSpec((rows, stack, lon_width), lambda i: (0, 0, i)),
            fixed(stack, modes),
        ),
        scratch_shapes=[pltpu.VMEM((2, 2 * rows * stack, HALF), BF16)],
        compiler_params=pltpu.CompilerParams(vmem_limit_bytes=VMEM_LIMIT),
        name="synthesis",
    )(arrived, table, eof_basis, eof_basis)
    grid = jnp.concatenate([first, last], axis=2).transpose(1, 0, 2)
    grid_fields = grid.reshape(members, fields, levels, rows, longitudes)
    share = modes // bands
    mem_count = lax.axis_size("mem")
    shares = partial.reshape(stack, bands, share).transpose(1, 0, 2)
    shares = jnp.broadcast_to(shares[:, None], (bands, mem_count, stack, share))
    shares = shares.reshape(bands * mem_count, stack, share)
    gathered = lax.all_to_all(shares, ("band", "mem"), split_axis=0, concat_axis=0, tiled=True)
    gathered = gathered.reshape(bands, mem_count, members, fields * levels, share)
    sums = jnp.sum(gathered, axis=0)
    mean = jnp.sum(sums, axis=(0, 1)) / (members * mem_count)
    own = lax.dynamic_index_in_dim(sums, lax.axis_index("mem"), 0, keepdims=False)
    anomaly = own - mean
    return (grid_fields, anomaly.reshape(members, fields, levels, share))


def solution(mesh):
    return jax.shard_map(
        shards,
        mesh=mesh,
        in_specs=(
            P("mem", None, None, None, "band"),
            P(None, "band"),
            P("band"),
            P(),
            P("band", None, None),
        ),
        out_specs=(P("mem", None, None, "band", None), P("mem", None, None, "band")),
        check_vma=False,
    )
```

```python
import math

import jax
import jax.numpy as jnp
import ml_dtypes
import numpy as np
from jax import lax
from jax.experimental import pallas as pl
from jax.experimental.pallas import tpu as pltpu
from jax.sharding import PartitionSpec as P

WAVE_COUNT = 1280
BLK = 128
HALF = WAVE_COUNT // 2
F32 = jnp.float32
BF16 = jnp.bfloat16
VMEM_LIMIT = 48 * 1024 * 1024
LEGENDRE_VMEM = 62 * 1024 * 1024


def iota(shape, axis):
    return lax.broadcasted_iota(jnp.int32, shape, axis)


def round_up(number, multiple):
    return -(-number // multiple) * multiple


def group_of(count, most):
    return max(size for size in range(1, most + 1) if count % size == 0)


def row_of(scalars, count, width):
    lane = iota((1, width), 1)
    values = jnp.zeros((1, width), jnp.int32)
    for index in range(count):
        values = jnp.where(lane == index, scalars[index], values)
    return values


def legendre_kernel(
    waves_smem, lengths_smem, spectra_ref, legendre_ref, out_ref, select_ref, total_ref,
    *, group, lat_half, lat_pad, bands, rows, pairs,
):
    step = pl.program_id(0)
    pair_len = legendre_ref.shape[1] // group
    fields = spectra_ref.shape[0]
    columns = 2 * fields
    width = 2 * rows * columns

    @pl.when(step == 0)
    def _():
        shape = (2 * rows * bands, 4 * lat_pad)
        slot = iota((2 * rows * bands, bands), 0)
        band = slot % bands
        lane = iota((2 * rows * bands, bands), 1)
        lengths = row_of(lengths_smem, bands, bands)
        start = jnp.sum(jnp.where(lane < band, lengths, 0).astype(F32), axis=1, keepdims=True)
        own = jnp.sum(jnp.where(lane == band, lengths, 0).astype(F32), axis=1, keepdims=True)
        slot = iota(shape, 0)
        row = slot // bands % rows
        place = iota(shape, 1)
        lat = jnp.broadcast_to(start, shape).astype(jnp.int32) + row
        keep = row < jnp.broadcast_to(own, shape).astype(jnp.int32)
        wanted = jnp.where(lat < lat_half, lat, lat_pad + 2 * lat_half - 1 - lat)
        wanted = wanted + slot // (bands * rows) * (2 * lat_pad)
        select_ref[...] = jnp.where(keep & (place == wanted), 1.0, 0.0).astype(BF16)

    widen = (iota((lat_pad, lat_half), 0) == iota((lat_pad, lat_half), 1)).astype(BF16)
    position = iota((lat_pad, pair_len), 1)
    sign = jnp.where(position % 2 == 0, 1.0, -1.0)
    lane_in = iota((width, width), 0)
    lane_out = iota((width, width), 1)
    block, rest = lane_in // columns, lane_in % columns
    target = ((block // rows * 2 + rest % 2) * rows + block % rows) * fields + rest // 2
    reorder = (lane_out == target).astype(BF16)
    north = jnp.dot(widen, legendre_ref[...], preferred_element_type=F32)
    sums = []
    for index in range(group):
        span = slice(index * pair_len, (index + 1) * pair_len)
        lower = waves_smem[step * group + index]
        high_start = WAVE_COUNT - lower // BLK * BLK
        low = position < WAVE_COUNT - lower
        high = (position >= high_start) & (position < high_start + lower + 1)
        low_part = jnp.where(low, north[:, span], 0.0)
        high_part = jnp.where(high, north[:, span], 0.0)
        weights = jnp.concatenate(
            [low_part, low_part * sign, high_part, high_part * sign], axis=0
        ).astype(BF16)
        coeffs = spectra_ref[:, :, span].reshape(columns, pair_len)
        sums.append(
            lax.dot_general(coeffs, weights, (((1,), (1,)), ((), ())), preferred_element_type=F32)
        )
    fourier = jnp.concatenate(sums, axis=0).astype(BF16)
    picked = lax.dot_general(
        select_ref[...], fourier, (((1,), (1,)), ((), ())), preferred_element_type=F32
    )
    wide = jnp.concatenate(
        [
            jnp.concatenate(
                [
                    picked[i * bands : (i + 1) * bands, index * columns : (index + 1) * columns]
                    for i in range(2 * rows)
                ],
                axis=1,
            )
            for index in range(group)
        ],
        axis=0,
    ).astype(BF16)
    wide = jnp.dot(wide, reorder, preferred_element_type=F32).reshape(group, bands, width)
    total_ref[pl.ds(step * group, group)] = wide

    @pl.when(step == pl.num_programs(0) - 1)
    def _():
        pad = out_ref.shape[1] - pairs
        waves = row_of(waves_smem, pairs, width)
        kind = iota((pad, width), 0)
        extra = jnp.where(
            kind == 0, (waves // BLK).astype(F32), jnp.where(kind == 1, (waves % BLK).astype(F32), 0.0)
        )
        total = jnp.swapaxes(total_ref[...], 0, 1)
        extra = jnp.broadcast_to(extra[None], (bands, pad, width))
        out_ref[...] = jnp.concatenate([total, extra], axis=1).astype(BF16)


def synthesis_kernel(
    payload_ref, table_ref, first_eof_ref, last_eof_ref, grid_ref, anomaly_ref,
    arrived_ref, waves_in_ref, projection_ref, shares_ref, shares_in_ref, members_ref,
    send_sem, recv_sem, share_send_sem, share_recv_sem, mem_send_sem, mem_recv_sem, local_sem,
    *, bands, mems, members, rows, pairs,
):
    step = pl.program_id(0)
    steps = pl.num_programs(0)
    taken = payload_ref.shape[1]
    width = payload_ref.shape[2]
    fields = width // (4 * rows)
    me = lax.axis_index("band")
    my_mem = lax.axis_index("mem")
    share = shares_ref.shape[1]

    def band_copies(source, landing, sends, receives):
        copies = []
        for hop in range(1, bands):
            peer = lax.rem(me + hop, bands)
            copies.append(
                pltpu.make_async_remote_copy(
                    src_ref=source.at[peer],
                    dst_ref=landing.at[me],
                    send_sem=sends.at[hop],
                    recv_sem=receives.at[hop],
                    device_id=(peer, my_mem),
                    device_id_type=pl.DeviceIdType.MESH,
                )
            )
        return copies

    @pl.when(step == 0)
    def _():
        barrier = pltpu.get_barrier_semaphore()
        for hop in range(1, bands):
            pl.semaphore_signal(
                barrier, inc=1, device_id=(lax.rem(me + hop, bands), my_mem),
                device_id_type=pl.DeviceIdType.MESH,
            )
        for hop in range(1, mems):
            pl.semaphore_signal(
                barrier, inc=1, device_id=(me, lax.rem(my_mem + hop, mems)),
                device_id_type=pl.DeviceIdType.MESH,
            )
        local = pltpu.make_async_copy(payload_ref.at[me], arrived_ref.at[me], local_sem)
        local.start()
        pl.semaphore_wait(barrier, bands + mems - 2)
        copies = band_copies(payload_ref, arrived_ref, send_sem, recv_sem)
        for copy in copies:
            copy.start()
        projection_ref[...] = jnp.zeros_like(projection_ref)
        local.wait()
        for copy in copies:
            copy.wait()
        count = bands * taken
        arrived = arrived_ref[...]
        coded = arrived.astype(F32)
        high = jnp.sum(jnp.where(iota(coded.shape, 1) == pairs, coded, 0.0), axis=1)
        low = jnp.sum(jnp.where(iota(coded.shape, 1) == pairs + 1, coded, 0.0), axis=1)
        waves = high * BLK + low
        waves = jnp.broadcast_to(waves[:, None, :], (bands, taken, width))
        slot = iota(waves.shape, 1)
        lane = iota(waves.shape, 2)
        own = jnp.sum(jnp.where(slot == lane, waves, 0.0), axis=2, keepdims=True)
        own = jnp.where(iota(own.shape, 1) < pairs, own, -1.0).reshape(count, 1)
        place = iota((count, HALF), 1)
        order = jnp.where(place < HALF // 2, 2 * place, 2 * place - (HALF - 1)).astype(F32)
        match = jnp.where(own == order, 1.0, 0.0).astype(BF16)
        ordered = lax.dot_general(
            arrived.reshape(count, width), match, (((0,), (0,)), ((), ())), preferred_element_type=F32
        )
        quarter = rows * fields
        first_half = iota((2 * quarter, HALF), 1) < HALF // 2
        low_order, high_order = ordered[: 2 * quarter], ordered[2 * quarter :]
        waves_in_ref[0] = jnp.where(first_half, low_order, high_order).astype(BF16)
        waves_in_ref[1] = jnp.where(first_half, high_order, low_order).astype(BF16)

    quarter = rows * fields
    even, odd = (
        jnp.dot(waves_in_ref[parity, :quarter], table_ref[parity, 0], preferred_element_type=F32)
        + jnp.dot(waves_in_ref[parity, quarter:], table_ref[parity, 1], preferred_element_type=F32)
        for parity in range(2)
    )
    total = projection_ref[...]
    lon_width = even.shape[1]
    for base, eof, value in ((0, first_eof_ref, even + odd), (steps, last_eof_ref, even - odd)):
        parts = [value[row * fields : (row + 1) * fields] for row in range(rows)]
        span = pl.ds(pl.multiple_of((base + step) * lon_width, lon_width), lon_width)
        grid_ref[:, :, span] = jnp.stack(parts, axis=1).astype(BF16)
        for row in range(rows):
            total += lax.dot_general(
                eof[row], parts[row].astype(BF16), (((0,), (1,)), ((), ())), preferred_element_type=F32
            )
    projection_ref[...] = total

    @pl.when(step == steps - 1)
    def _():
        shares_ref[...] = projection_ref[...].reshape(bands, share, fields)
        copies = band_copies(shares_ref, shares_in_ref, share_send_sem, share_recv_sem)
        for copy in copies:
            copy.start()
        shares_in_ref[me] = shares_ref[me]
        for copy in copies:
            copy.wait()
        own = jnp.sum(shares_in_ref[...], axis=0)
        members_ref[my_mem] = own
        copies = []
        for hop in range(1, mems):
            peer = lax.rem(my_mem + hop, mems)
            copies.append(
                pltpu.make_async_remote_copy(
                    src_ref=members_ref.at[my_mem],
                    dst_ref=members_ref.at[my_mem],
                    send_sem=mem_send_sem.at[hop],
                    recv_sem=mem_recv_sem.at[hop],
                    device_id=(me, peer),
                    device_id_type=pl.DeviceIdType.MESH,
                )
            )
        for copy in copies:
            copy.start()
        for copy in copies:
            copy.wait()
        total = jnp.sum(members_ref[...], axis=0)
        stack = fields // members
        mean = sum(total[:, i * stack : (i + 1) * stack] for i in range(members)) / (members * mems)
        anomaly_ref[...] = own - jnp.concatenate([mean] * members, axis=1)


def wave_tables(longitudes):
    place = np.arange(HALF)
    lower = np.where(place < HALF // 2, 2 * place, 2 * place - (HALF - 1))
    upper = WAVE_COUNT - 1 - lower
    even = np.where(lower % 2 == 0, lower, upper)
    orders = np.stack([even, WAVE_COUNT - 1 - even])
    phase = orders[..., None] * np.arange(longitudes // 2) % longitudes
    angle = phase * (2.0 * math.pi / longitudes)
    weight = np.where(orders == 0, 1.0, 2.0)[..., None]
    table = np.stack([weight * np.cos(angle), -weight * np.sin(angle)], axis=1)
    return table.astype(np.float32).astype(ml_dtypes.bfloat16)


def shards(spectra, legendre, pair_waves, band_lengths, eof_basis):
    members, fields, levels, re_im, slot_count = spectra.shape
    lat_half = legendre.shape[0]
    pairs = pair_waves.shape[0]
    pair_len = slot_count // pairs
    stack = members * fields * levels
    bands = lax.axis_size("band")
    rows, longitudes, modes = eof_basis.shape
    width = 2 * rows * stack * re_im
    group = group_of(pairs, 8)
    lat_pad = round_up(lat_half, 16)
    taken = round_up(pairs + 2, 16)
    mems = lax.axis_size("mem")

    def fixed(*shape):
        return pl.BlockSpec(shape, lambda *_: (0,) * len(shape))

    payload = pl.pallas_call(
        lambda *refs: legendre_kernel(
            *refs, group=group, lat_half=lat_half, lat_pad=lat_pad, bands=bands, rows=rows, pairs=pairs
        ),
        out_shape=jax.ShapeDtypeStruct((bands, taken, width), BF16),
        grid_spec=pltpu.PrefetchScalarGridSpec(
            num_scalar_prefetch=2,
            grid=(pairs // group,),
            in_specs=[
                pl.BlockSpec((stack, re_im, group * pair_len), lambda i, *_: (0, 0, i)),
                pl.BlockSpec((lat_half, group * pair_len), lambda i, *_: (0, i)),
            ],
            out_specs=fixed(bands, taken, width),
            scratch_shapes=[
                pltpu.VMEM((2 * rows * bands, 4 * lat_pad), BF16),
                pltpu.VMEM((pairs, bands, width), F32),
            ],
        ),
        compiler_params=pltpu.CompilerParams(vmem_limit_bytes=LEGENDRE_VMEM),
        name="legendre",
    )(pair_waves, band_lengths, spectra.reshape(stack, re_im, slot_count), legendre)
    lon_width = math.gcd(longitudes // 2, 256)
    steps = longitudes // 2 // lon_width
    table = jnp.asarray(wave_tables(longitudes))
    share = modes // bands
    dma = pltpu.SemaphoreType.DMA
    grid, anomaly = pl.pallas_call(
        lambda *refs: synthesis_kernel(
            *refs, bands=bands, mems=mems, members=members, rows=rows, pairs=pairs
        ),
        out_shape=(
            jax.ShapeDtypeStruct((stack, rows, longitudes), BF16),
            jax.ShapeDtypeStruct((share, stack), F32),
        ),
        grid=(steps,),
        in_specs=[
            fixed(bands, taken, width),
            pl.BlockSpec((2, 2, HALF, lon_width), lambda i: (0, 0, 0, i)),
            pl.BlockSpec((rows, lon_width, modes), lambda i: (0, i, 0)),
            pl.BlockSpec((rows, lon_width, modes), lambda i: (0, i + steps, 0)),
        ],
        out_specs=(fixed(stack, rows, longitudes), fixed(share, stack)),
        scratch_shapes=[
            pltpu.VMEM((bands, taken, width), BF16),
            pltpu.VMEM((2, 2 * rows * stack, HALF), BF16),
            pltpu.VMEM((modes, stack), F32),
            pltpu.VMEM((bands, share, stack), F32),
            pltpu.VMEM((bands, share, stack), F32),
            pltpu.VMEM((mems, share, stack), F32),
            dma((bands,)),
            dma((bands,)),
            dma((bands,)),
            dma((bands,)),
            dma((mems,)),
            dma((mems,)),
            dma,
        ],
        compiler_params=pltpu.CompilerParams(
            vmem_limit_bytes=VMEM_LIMIT, collective_id=0, has_side_effects=True
        ),
        name="synthesis",
    )(payload, table, eof_basis, eof_basis)
    grid_fields = grid.reshape(members, fields, levels, rows, longitudes)
    return (grid_fields, anomaly.T.reshape(members, fields, levels, share))


def solution(mesh):
    return jax.shard_map(
        shards,
        mesh=mesh,
        in_specs=(
            P("mem", None, None, None, "band"),
            P(None, "band"),
            P("band"),
            P(),
            P("band", None, None),
        ),
        out_specs=(P("mem", None, None, "band", None), P("mem", None, None, "band")),
        check_vma=False,
    )
```

```python
import math

import jax
import jax.numpy as jnp
import ml_dtypes
import numpy as np
from jax import lax
from jax.experimental import pallas as pl
from jax.experimental.pallas import tpu as pltpu
from jax.sharding import PartitionSpec as P

WAVE_COUNT = 1280
BLK = 128
HALF = WAVE_COUNT // 2
F32 = jnp.float32
BF16 = jnp.bfloat16
VMEM_LIMIT = 62 * 1024 * 1024


def iota(shape, axis):
    return lax.broadcasted_iota(jnp.int32, shape, axis)


def round_up(number, multiple):
    return -(-number // multiple) * multiple


def group_of(count, most):
    return max(size for size in range(1, most + 1) if count % size == 0)


def row_of(scalars, count, width):
    lane = iota((1, width), 1)
    values = jnp.zeros((1, width), jnp.int32)
    for index in range(count):
        values = jnp.where(lane == index, scalars[index], values)
    return values


def transform_kernel(
    waves_smem, lengths_smem, spectra_ref, legendre_ref, table_hbm, eof_hbm, grid_ref, anomaly_ref,
    select_ref, total_ref, payload_ref, arrived_ref, waves_in_ref, projection_ref,
    shares_ref, shares_in_ref, members_ref, table_ref, eof_ref,
    send_sem, recv_sem, share_send_sem, share_recv_sem, mem_send_sem, mem_recv_sem, local_sem,
    *, group, lat_half, lat_pad, bands, mems, members, rows, pairs, lon_width,
):
    step = pl.program_id(0)
    steps = pl.num_programs(0)
    pair_steps = pairs // group
    pair_len = legendre_ref.shape[1] // group
    fields = spectra_ref.shape[0]
    columns = 2 * fields
    width = 2 * rows * columns
    quarter = rows * fields
    taken = payload_ref.shape[1]
    me = lax.axis_index("band")
    my_mem = lax.axis_index("mem")
    table_copy = pltpu.make_async_copy(table_hbm, table_ref, local_sem.at[0])
    eof_copy = pltpu.make_async_copy(eof_hbm, eof_ref, local_sem.at[1])

    def band_copies(source, landing, sends, receives):
        copies = []
        for hop in range(1, bands):
            peer = lax.rem(me + hop, bands)
            copies.append(
                pltpu.make_async_remote_copy(
                    src_ref=source.at[peer],
                    dst_ref=landing.at[me],
                    send_sem=sends.at[hop],
                    recv_sem=receives.at[hop],
                    device_id=(peer, my_mem),
                    device_id_type=pl.DeviceIdType.MESH,
                )
            )
        return copies

    @pl.when(step == 0)
    def _():
        barrier = pltpu.get_barrier_semaphore()
        for hop in range(1, bands):
            pl.semaphore_signal(
                barrier, inc=1, device_id=(lax.rem(me + hop, bands), my_mem),
                device_id_type=pl.DeviceIdType.MESH,
            )
        for hop in range(1, mems):
            pl.semaphore_signal(
                barrier, inc=1, device_id=(me, lax.rem(my_mem + hop, mems)),
                device_id_type=pl.DeviceIdType.MESH,
            )
        table_copy.start()
        eof_copy.start()
        shape = (2 * rows * bands, 4 * lat_pad)
        slot = iota((2 * rows * bands, bands), 0)
        band = slot % bands
        lane = iota((2 * rows * bands, bands), 1)
        lengths = row_of(lengths_smem, bands, bands)
        start = jnp.sum(jnp.where(lane < band, lengths, 0).astype(F32), axis=1, keepdims=True)
        own = jnp.sum(jnp.where(lane == band, lengths, 0).astype(F32), axis=1, keepdims=True)
        slot = iota(shape, 0)
        row = slot // bands % rows
        place = iota(shape, 1)
        lat = jnp.broadcast_to(start, shape).astype(jnp.int32) + row
        keep = row < jnp.broadcast_to(own, shape).astype(jnp.int32)
        wanted = jnp.where(lat < lat_half, lat, lat_pad + 2 * lat_half - 1 - lat)
        wanted = wanted + slot // (bands * rows) * (2 * lat_pad)
        select_ref[...] = jnp.where(keep & (place == wanted), 1.0, 0.0).astype(BF16)

    @pl.when(step < pair_steps)
    def _():
        widen = (iota((lat_pad, lat_half), 0) == iota((lat_pad, lat_half), 1)).astype(BF16)
        position = iota((lat_pad, pair_len), 1)
        sign = jnp.where(position % 2 == 0, 1.0, -1.0)
        lane_in = iota((width, width), 0)
        lane_out = iota((width, width), 1)
        block, rest = lane_in // columns, lane_in % columns
        target = ((block // rows * 2 + rest % 2) * rows + block % rows) * fields + rest // 2
        reorder = (lane_out == target).astype(BF16)
        north = jnp.dot(widen, legendre_ref[...], preferred_element_type=F32)
        sums = []
        for index in range(group):
            span = slice(index * pair_len, (index + 1) * pair_len)
            lower = waves_smem[step * group + index]
            high_start = WAVE_COUNT - lower // BLK * BLK
            low = position < WAVE_COUNT - lower
            high = (position >= high_start) & (position < high_start + lower + 1)
            low_part = jnp.where(low, north[:, span], 0.0)
            high_part = jnp.where(high, north[:, span], 0.0)
            weights = jnp.concatenate(
                [low_part, low_part * sign, high_part, high_part * sign], axis=0
            ).astype(BF16)
            coeffs = spectra_ref[:, :, span].reshape(columns, pair_len)
            sums.append(
                lax.dot_general(coeffs, weights, (((1,), (1,)), ((), ())), preferred_element_type=F32)
            )
        fourier = jnp.concatenate(sums, axis=0).astype(BF16)
        picked = lax.dot_general(
            select_ref[...], fourier, (((1,), (1,)), ((), ())), preferred_element_type=F32
        )
        wide = jnp.concatenate(
            [
                jnp.concatenate(
                    [
                        picked[i * bands : (i + 1) * bands, index * columns : (index + 1) * columns]
                        for i in range(2 * rows)
                    ],
                    axis=1,
                )
                for index in range(group)
            ],
            axis=0,
        ).astype(BF16)
        wide = jnp.dot(wide, reorder, preferred_element_type=F32).reshape(group, bands, width)
        total_ref[pl.ds(step * group, group)] = wide

    @pl.when(step == pair_steps - 1)
    def _():
        pad = payload_ref.shape[1] - pairs
        waves = row_of(waves_smem, pairs, width)
        kind = iota((pad, width), 0)
        extra = jnp.where(
            kind == 0, (waves // BLK).astype(F32), jnp.where(kind == 1, (waves % BLK).astype(F32), 0.0)
        )
        total = jnp.swapaxes(total_ref[...], 0, 1)
        extra = jnp.broadcast_to(extra[None], (bands, pad, width))
        payload_ref[...] = jnp.concatenate([total, extra], axis=1).astype(BF16)
        pl.semaphore_wait(pltpu.get_barrier_semaphore(), bands + mems - 2)
        copies = band_copies(payload_ref, arrived_ref, send_sem, recv_sem)
        for copy in copies:
            copy.start()
        arrived_ref[me] = payload_ref[me]
        projection_ref[...] = jnp.zeros_like(projection_ref)
        for copy in copies:
            copy.wait()
        count = bands * taken
        arrived = arrived_ref[...]
        coded = arrived.astype(F32)
        high = jnp.sum(jnp.where(iota(coded.shape, 1) == pairs, coded, 0.0), axis=1)
        low = jnp.sum(jnp.where(iota(coded.shape, 1) == pairs + 1, coded, 0.0), axis=1)
        waves = high * BLK + low
        waves = jnp.broadcast_to(waves[:, None, :], (bands, taken, width))
        slot = iota(waves.shape, 1)
        lane = iota(waves.shape, 2)
        own = jnp.sum(jnp.where(slot == lane, waves, 0.0), axis=2, keepdims=True)
        own = jnp.where(iota(own.shape, 1) < pairs, own, -1.0).reshape(count, 1)
        place = iota((count, HALF), 1)
        order = jnp.where(place < HALF // 2, 2 * place, 2 * place - (HALF - 1)).astype(F32)
        match = jnp.where(own == order, 1.0, 0.0).astype(BF16)
        ordered = lax.dot_general(
            arrived.reshape(count, width), match, (((0,), (0,)), ((), ())), preferred_element_type=F32
        )
        first_half = iota((2 * quarter, HALF), 1) < HALF // 2
        low_order, high_order = ordered[: 2 * quarter], ordered[2 * quarter :]
        waves_in_ref[0] = jnp.where(first_half, low_order, high_order).astype(BF16)
        waves_in_ref[1] = jnp.where(first_half, high_order, low_order).astype(BF16)
        table_copy.wait()
        eof_copy.wait()

    @pl.when(step >= pair_steps)
    def _():
        place = step - pair_steps
        span = pl.ds(pl.multiple_of(place * lon_width, lon_width), lon_width)
        even, odd = (
            jnp.dot(
                waves_in_ref[parity, :quarter], table_ref[parity, 0, :, span],
                preferred_element_type=F32,
            )
            + jnp.dot(
                waves_in_ref[parity, quarter:], table_ref[parity, 1, :, span],
                preferred_element_type=F32,
            )
            for parity in range(2)
        )
        total = projection_ref[...]
        for base, value in ((0, even + odd), (steps - pair_steps, even - odd)):
            parts = [value[row * fields : (row + 1) * fields] for row in range(rows)]
            span = pl.ds(pl.multiple_of((base + place) * lon_width, lon_width), lon_width)
            grid_ref[:, :, span] = jnp.stack(parts, axis=1).astype(BF16)
            for row in range(rows):
                total += lax.dot_general(
                    eof_ref[row, span, :], parts[row].astype(BF16), (((0,), (1,)), ((), ())),
                    preferred_element_type=F32,
                )
        projection_ref[...] = total

    @pl.when(step == steps - 1)
    def _():
        fold = shares_ref.shape[2] // fields
        high = shares_ref.shape[1]
        shares = projection_ref[...].reshape(bands, fold * high, fields)
        shares_ref[...] = jnp.concatenate(
            [shares[:, i * high : (i + 1) * high] for i in range(fold)], axis=2
        )
        copies = band_copies(shares_ref, shares_in_ref, share_send_sem, share_recv_sem)
        for copy in copies:
            copy.start()
        shares_in_ref[me] = shares_ref[me]
        for copy in copies:
            copy.wait()
        own = jnp.sum(shares_in_ref[...], axis=0)
        members_ref[my_mem] = own
        copies = []
        for hop in range(1, mems):
            peer = lax.rem(my_mem + hop, mems)
            copies.append(
                pltpu.make_async_remote_copy(
                    src_ref=members_ref.at[my_mem],
                    dst_ref=members_ref.at[my_mem],
                    send_sem=mem_send_sem.at[hop],
                    recv_sem=mem_recv_sem.at[hop],
                    device_id=(me, peer),
                    device_id_type=pl.DeviceIdType.MESH,
                )
            )
        for copy in copies:
            copy.start()
        for copy in copies:
            copy.wait()

        def unfolded(value):
            return jnp.concatenate(
                [value[:, i * fields : (i + 1) * fields] for i in range(fold)], axis=0
            )

        total = unfolded(jnp.sum(members_ref[...], axis=0))
        stack = fields // members
        mean = sum(total[:, i * stack : (i + 1) * stack] for i in range(members)) / (members * mems)
        anomaly_ref[...] = unfolded(own) - jnp.concatenate([mean] * members, axis=1)


def wave_tables(longitudes):
    place = np.arange(HALF)
    lower = np.where(place < HALF // 2, 2 * place, 2 * place - (HALF - 1))
    upper = WAVE_COUNT - 1 - lower
    even = np.where(lower % 2 == 0, lower, upper)
    orders = np.stack([even, WAVE_COUNT - 1 - even])
    phase = orders[..., None] * np.arange(longitudes // 2) % longitudes
    angle = phase * (2.0 * math.pi / longitudes)
    weight = np.where(orders == 0, 1.0, 2.0)[..., None]
    table = np.stack([weight * np.cos(angle), -weight * np.sin(angle)], axis=1)
    return table.astype(np.float32).astype(ml_dtypes.bfloat16)


def shards(spectra, legendre, pair_waves, band_lengths, eof_basis):
    members, fields, levels, re_im, slot_count = spectra.shape
    lat_half = legendre.shape[0]
    pairs = pair_waves.shape[0]
    pair_len = slot_count // pairs
    stack = members * fields * levels
    bands = lax.axis_size("band")
    rows, longitudes, modes = eof_basis.shape
    width = 2 * rows * stack * re_im
    group = group_of(pairs, 8)
    lat_pad = round_up(lat_half, 16)
    taken = round_up(pairs + 2, 16)
    mems = lax.axis_size("mem")

    def fixed(*shape):
        return pl.BlockSpec(shape, lambda *_: (0,) * len(shape))

    lon_width = math.gcd(longitudes // 2, 256)
    pair_steps = pairs // group
    table = wave_tables(longitudes)
    share = modes // bands
    fold = max(1, share // 8)
    folded = (share // fold, fold * stack)
    dma = pltpu.SemaphoreType.DMA
    grid, anomaly = pl.pallas_call(
        lambda *refs: transform_kernel(
            *refs, group=group, lat_half=lat_half, lat_pad=lat_pad, bands=bands, mems=mems,
            members=members, rows=rows, pairs=pairs, lon_width=lon_width,
        ),
        out_shape=(
            jax.ShapeDtypeStruct((stack, rows, longitudes), BF16),
            jax.ShapeDtypeStruct((share, stack), F32),
        ),
        grid=(pair_steps + longitudes // 2 // lon_width,),
        in_specs=[
            pl.BlockSpec(memory_space=pltpu.SMEM),
            pl.BlockSpec(memory_space=pltpu.SMEM),
            pl.BlockSpec(
                (stack, re_im, group * pair_len), lambda i: (0, 0, jnp.minimum(i, pair_steps - 1))
            ),
            pl.BlockSpec((lat_half, group * pair_len), lambda i: (0, jnp.minimum(i, pair_steps - 1))),
            pl.BlockSpec(memory_space=pl.ANY),
            pl.BlockSpec(memory_space=pl.ANY),
        ],
        out_specs=(fixed(stack, rows, longitudes), fixed(share, stack)),
        scratch_shapes=[
            pltpu.VMEM((2 * rows * bands, 4 * lat_pad), BF16),
            pltpu.VMEM((pairs, bands, width), F32),
            pltpu.VMEM((bands, taken, width), BF16),
            pltpu.VMEM((bands, taken, width), BF16),
            pltpu.VMEM((2, 2 * rows * stack, HALF), BF16),
            pltpu.VMEM((modes, stack), F32),
            pltpu.VMEM((bands, *folded), F32),
            pltpu.VMEM((bands, *folded), F32),
            pltpu.VMEM((mems, *folded), F32),
            pltpu.VMEM(table.shape, BF16),
            pltpu.VMEM(eof_basis.shape, BF16),
            dma((bands,)),
            dma((bands,)),
            dma((bands,)),
            dma((bands,)),
            dma((mems,)),
            dma((mems,)),
            dma((2,)),
        ],
        compiler_params=pltpu.CompilerParams(
            vmem_limit_bytes=VMEM_LIMIT, collective_id=0, has_side_effects=True
        ),
        name="transform",
    )(
        pair_waves,
        band_lengths,
        spectra.reshape(stack, re_im, slot_count),
        legendre,
        jnp.asarray(table),
        eof_basis,
    )
    grid_fields = grid.reshape(members, fields, levels, rows, longitudes)
    return (grid_fields, anomaly.T.reshape(members, fields, levels, share))


def solution(mesh):
    return jax.shard_map(
        shards,
        mesh=mesh,
        in_specs=(
            P("mem", None, None, None, "band"),
            P(None, "band"),
            P("band"),
            P(),
            P("band", None, None),
        ),
        out_specs=(P("mem", None, None, "band", None), P("mem", None, None, "band")),
        check_vma=False,
    )
```

```python
import math

import jax
import jax.numpy as jnp
import ml_dtypes
import numpy as np
from jax import lax
from jax.experimental import pallas as pl
from jax.experimental.pallas import tpu as pltpu
from jax.sharding import PartitionSpec as P

WAVE_COUNT = 1280
BLK = 128
HALF = WAVE_COUNT // 2
F32 = jnp.float32
BF16 = jnp.bfloat16
VMEM_LIMIT = 58 * 1024 * 1024


def iota(shape, axis):
    return lax.broadcasted_iota(jnp.int32, shape, axis)


def round_up(number, multiple):
    return -(-number // multiple) * multiple


def group_of(count, most):
    return max(size for size in range(1, most + 1) if count % size == 0)


def row_of(scalars, count, width):
    lane = iota((1, width), 1)
    values = jnp.zeros((1, width), jnp.int32)
    for index in range(count):
        values = jnp.where(lane == index, scalars[index], values)
    return values


def transform_kernel(
    waves_smem, lengths_smem, spectra_hbm, legendre_hbm, table_hbm, eof_hbm, grid_ref, anomaly_ref,
    spectra_ref, legendre_ref, select_ref, total_ref, first_out_ref, first_in_ref, last_out_ref, last_in_ref,
    waves_in_ref, projection_ref,
    shares_ref, shares_in_ref, members_ref, table_ref, eof_ref,
    first_send_sem, first_recv_sem, last_send_sem, last_recv_sem, share_send_sem, share_recv_sem,
    mem_send_sem, mem_recv_sem, local_sem, input_sem,
    *, group, lat_half, lat_pad, bands, mems, members, rows, pairs, lon_width, first_steps,
):
    step = pl.program_id(0)
    steps = pl.num_programs(0)
    pair_steps = pairs // group
    span_len = legendre_ref.shape[2]
    pair_len = span_len // group
    fields = spectra_ref.shape[1]
    first_pairs = first_steps * group
    columns = 2 * fields
    width = 2 * rows * columns
    quarter = rows * fields
    me = lax.axis_index("band")
    my_mem = lax.axis_index("mem")
    table_copy = pltpu.make_async_copy(table_hbm, table_ref, local_sem.at[0])
    eof_copy = pltpu.make_async_copy(eof_hbm, eof_ref, local_sem.at[1])

    def input_copies(index):
        span = pl.ds(pl.multiple_of(index * span_len, BLK), span_len)
        return (
            pltpu.make_async_copy(
                spectra_hbm.at[:, :, span], spectra_ref.at[index], input_sem.at[0, index]
            ),
            pltpu.make_async_copy(
                legendre_hbm.at[:, span], legendre_ref.at[index], input_sem.at[1, index]
            ),
        )

    def band_copies(source, landing, sends, receives):
        copies = []
        for hop in range(1, bands):
            peer = lax.rem(me + hop, bands)
            copies.append(
                pltpu.make_async_remote_copy(
                    src_ref=source.at[peer],
                    dst_ref=landing.at[me],
                    send_sem=sends.at[hop],
                    recv_sem=receives.at[hop],
                    device_id=(peer, my_mem),
                    device_id_type=pl.DeviceIdType.MESH,
                )
            )
        return copies

    @pl.when(step == 0)
    def _():
        for index in range(pair_steps):
            for copy in input_copies(index):
                copy.start()
        barrier = pltpu.get_barrier_semaphore()
        for hop in range(1, bands):
            pl.semaphore_signal(
                barrier, inc=1, device_id=(lax.rem(me + hop, bands), my_mem),
                device_id_type=pl.DeviceIdType.MESH,
            )
        for hop in range(1, mems):
            pl.semaphore_signal(
                barrier, inc=1, device_id=(me, lax.rem(my_mem + hop, mems)),
                device_id_type=pl.DeviceIdType.MESH,
            )
        table_copy.start()
        eof_copy.start()
        shape = (2 * rows * bands, 4 * lat_pad)
        slot = iota((2 * rows * bands, bands), 0)
        band = slot % bands
        lane = iota((2 * rows * bands, bands), 1)
        lengths = row_of(lengths_smem, bands, bands)
        start = jnp.sum(jnp.where(lane < band, lengths, 0).astype(F32), axis=1, keepdims=True)
        own = jnp.sum(jnp.where(lane == band, lengths, 0).astype(F32), axis=1, keepdims=True)
        slot = iota(shape, 0)
        row = slot // bands % rows
        place = iota(shape, 1)
        lat = jnp.broadcast_to(start, shape).astype(jnp.int32) + row
        keep = row < jnp.broadcast_to(own, shape).astype(jnp.int32)
        wanted = jnp.where(lat < lat_half, lat, lat_pad + 2 * lat_half - 1 - lat)
        wanted = wanted + slot // (bands * rows) * (2 * lat_pad)
        select_ref[...] = jnp.where(keep & (place == wanted), 1.0, 0.0).astype(BF16)

    @pl.when(step < pair_steps)
    def _():
        for copy in input_copies(step):
            copy.wait()
        position = iota((lat_pad, pair_len), 1)
        sign = jnp.where(position % 2 == 0, 1.0, -1.0)
        lane_in = iota((width, width), 0)
        lane_out = iota((width, width), 1)
        block, rest = lane_in // columns, lane_in % columns
        target = ((block // rows * 2 + rest % 2) * rows + block % rows) * fields + rest // 2
        reorder = (lane_out == target).astype(BF16)
        sums = []
        for index in range(group):
            span = slice(index * pair_len, (index + 1) * pair_len)
            lower = waves_smem[step * group + index]
            high_start = WAVE_COUNT - lower // BLK * BLK
            low = position < WAVE_COUNT - lower
            high = (position >= high_start) & (position < high_start + lower + 1)
            north = legendre_ref[step, :, span].astype(F32)
            north = jnp.concatenate(
                [north, jnp.zeros((lat_pad - lat_half, pair_len), F32)], axis=0
            )
            low_part = jnp.where(low, north, 0.0)
            high_part = jnp.where(high, north, 0.0)
            weights = jnp.concatenate(
                [low_part, low_part * sign, high_part, high_part * sign], axis=0
            ).astype(BF16)
            coeffs = spectra_ref[step, :, :, span].reshape(columns, pair_len)
            sums.append(
                lax.dot_general(coeffs, weights, (((1,), (1,)), ((), ())), preferred_element_type=F32)
            )
        fourier = jnp.concatenate(sums, axis=0).astype(BF16)
        picked = lax.dot_general(
            select_ref[...], fourier, (((1,), (1,)), ((), ())), preferred_element_type=F32
        )
        wide = jnp.concatenate(
            [
                jnp.concatenate(
                    [
                        picked[i * bands : (i + 1) * bands, index * columns : (index + 1) * columns]
                        for i in range(2 * rows)
                    ],
                    axis=1,
                )
                for index in range(group)
            ],
            axis=0,
        ).astype(BF16)
        wide = jnp.dot(wide, reorder, preferred_element_type=F32).reshape(group, bands, width)
        total_ref[pl.ds(step * group, group)] = wide

    first_copies = band_copies(first_out_ref, first_in_ref, first_send_sem, first_recv_sem)

    @pl.when(step == first_steps - 1)
    def _():
        pad = first_out_ref.shape[1] - first_pairs
        waves = row_of(waves_smem, pairs, width)
        kind = iota((pad, width), 0)
        extra = jnp.where(
            kind == 0, (waves // BLK).astype(F32), jnp.where(kind == 1, (waves % BLK).astype(F32), 0.0)
        )
        total = jnp.swapaxes(total_ref[:first_pairs], 0, 1)
        extra = jnp.broadcast_to(extra[None], (bands, pad, width))
        first_out_ref[...] = jnp.concatenate([total, extra], axis=1).astype(BF16)
        pl.semaphore_wait(pltpu.get_barrier_semaphore(), bands + mems - 2)
        for copy in first_copies:
            copy.start()
        first_in_ref[me] = first_out_ref[me]

    @pl.when(step == pair_steps - 1)
    def _():
        total = jnp.swapaxes(total_ref[first_pairs:], 0, 1)
        pad = last_out_ref.shape[1] - (pairs - first_pairs)
        if pad:
            total = jnp.concatenate([total, jnp.zeros((bands, pad, width), F32)], axis=1)
        last_out_ref[...] = total.astype(BF16)
        last_copies = band_copies(last_out_ref, last_in_ref, last_send_sem, last_recv_sem)
        for copy in last_copies:
            copy.start()
        last_in_ref[me] = last_out_ref[me]
        projection_ref[...] = jnp.zeros_like(projection_ref)
        for copy in first_copies:
            copy.wait()
        arrived = first_in_ref[...]
        coded = arrived[:, first_pairs:].astype(F32)
        high = jnp.sum(jnp.where(iota(coded.shape, 1) == 0, coded, 0.0), axis=1)
        low = jnp.sum(jnp.where(iota(coded.shape, 1) == 1, coded, 0.0), axis=1)
        waves = high * BLK + low

        def match_of(offset, held, taken):
            spread = jnp.broadcast_to(waves[:, None, :], (bands, taken, width))
            slot = iota(spread.shape, 1)
            lane = iota(spread.shape, 2)
            own = jnp.sum(jnp.where(slot + offset == lane, spread, 0.0), axis=2, keepdims=True)
            own = jnp.where(iota(own.shape, 1) < held, own, -1.0).reshape(bands * taken, 1)
            place = iota((bands * taken, HALF), 1)
            order = jnp.where(place < HALF // 2, 2 * place, 2 * place - (HALF - 1)).astype(F32)
            return jnp.where(own == order, 1.0, 0.0).astype(BF16)

        def placed(values, match):
            return lax.dot_general(
                values.reshape(match.shape[0], width), match, (((0,), (0,)), ((), ())),
                preferred_element_type=F32,
            )

        first_match = match_of(0, first_pairs, first_in_ref.shape[1])
        last_match = match_of(first_pairs, pairs - first_pairs, last_in_ref.shape[1])
        ordered = placed(arrived, first_match)
        for copy in last_copies:
            copy.wait()
        ordered += placed(last_in_ref[...], last_match)
        first_half = iota((2 * quarter, HALF), 1) < HALF // 2
        low_order, high_order = ordered[: 2 * quarter], ordered[2 * quarter :]
        waves_in_ref[0] = jnp.where(first_half, low_order, high_order).astype(BF16)
        waves_in_ref[1] = jnp.where(first_half, high_order, low_order).astype(BF16)
        table_copy.wait()
        eof_copy.wait()

    @pl.when(step >= pair_steps)
    def _():
        place = step - pair_steps
        span = pl.ds(pl.multiple_of(place * lon_width, lon_width), lon_width)
        even, odd = (
            jnp.dot(
                waves_in_ref[parity, :quarter], table_ref[parity, 0, :, span],
                preferred_element_type=F32,
            )
            + jnp.dot(
                waves_in_ref[parity, quarter:], table_ref[parity, 1, :, span],
                preferred_element_type=F32,
            )
            for parity in range(2)
        )
        total = projection_ref[...]
        for base, value in ((0, even + odd), (steps - pair_steps, even - odd)):
            parts = [value[row * fields : (row + 1) * fields] for row in range(rows)]
            span = pl.ds(pl.multiple_of((base + place) * lon_width, lon_width), lon_width)
            grid_ref[:, :, span] = jnp.stack(parts, axis=1).astype(BF16)
            for row in range(rows):
                total += lax.dot_general(
                    eof_ref[row, span, :], parts[row].astype(BF16), (((0,), (1,)), ((), ())),
                    preferred_element_type=F32,
                )
        projection_ref[...] = total

    @pl.when(step == steps - 1)
    def _():
        fold = shares_ref.shape[2] // fields
        high = shares_ref.shape[1]
        shares = projection_ref[...].reshape(bands, fold * high, fields)
        shares_ref[...] = jnp.concatenate(
            [shares[:, i * high : (i + 1) * high] for i in range(fold)], axis=2
        )
        copies = band_copies(shares_ref, shares_in_ref, share_send_sem, share_recv_sem)
        for copy in copies:
            copy.start()
        shares_in_ref[me] = shares_ref[me]
        for copy in copies:
            copy.wait()
        own = jnp.sum(shares_in_ref[...], axis=0)
        members_ref[my_mem] = own
        copies = []
        for hop in range(1, mems):
            peer = lax.rem(my_mem + hop, mems)
            copies.append(
                pltpu.make_async_remote_copy(
                    src_ref=members_ref.at[my_mem],
                    dst_ref=members_ref.at[my_mem],
                    send_sem=mem_send_sem.at[hop],
                    recv_sem=mem_recv_sem.at[hop],
                    device_id=(me, peer),
                    device_id_type=pl.DeviceIdType.MESH,
                )
            )
        for copy in copies:
            copy.start()
        for copy in copies:
            copy.wait()

        def unfolded(value):
            return jnp.concatenate(
                [value[:, i * fields : (i + 1) * fields] for i in range(fold)], axis=0
            )

        total = unfolded(jnp.sum(members_ref[...], axis=0))
        stack = fields // members
        mean = sum(total[:, i * stack : (i + 1) * stack] for i in range(members)) / (members * mems)
        anomaly_ref[...] = unfolded(own) - jnp.concatenate([mean] * members, axis=1)


def wave_tables(longitudes):
    place = np.arange(HALF)
    lower = np.where(place < HALF // 2, 2 * place, 2 * place - (HALF - 1))
    upper = WAVE_COUNT - 1 - lower
    even = np.where(lower % 2 == 0, lower, upper)
    orders = np.stack([even, WAVE_COUNT - 1 - even])
    phase = orders[..., None] * np.arange(longitudes // 2) % longitudes
    angle = phase * (2.0 * math.pi / longitudes)
    weight = np.where(orders == 0, 1.0, 2.0)[..., None]
    table = np.stack([weight * np.cos(angle), -weight * np.sin(angle)], axis=1)
    return table.astype(np.float32).astype(ml_dtypes.bfloat16)


def shards(spectra, legendre, pair_waves, band_lengths, eof_basis):
    members, fields, levels, re_im, slot_count = spectra.shape
    lat_half = legendre.shape[0]
    pairs = pair_waves.shape[0]
    pair_len = slot_count // pairs
    stack = members * fields * levels
    bands = lax.axis_size("band")
    rows, longitudes, modes = eof_basis.shape
    width = 2 * rows * stack * re_im
    group = group_of(pairs, 8)
    lat_pad = round_up(lat_half, 16)
    mems = lax.axis_size("mem")

    def fixed(*shape):
        return pl.BlockSpec(shape, lambda *_: (0,) * len(shape))

    lon_width = math.gcd(longitudes // 2, 256)
    pair_steps = pairs // group
    first_steps = (pair_steps + 1) // 2
    first_pairs = first_steps * group
    first_shape = (bands, round_up(first_pairs + 2, 16), width)
    last_shape = (bands, round_up(pairs - first_pairs, 16), width)
    table = wave_tables(longitudes)
    share = modes // bands
    fold = max(1, share // 8)
    folded = (share // fold, fold * stack)
    dma = pltpu.SemaphoreType.DMA
    grid, anomaly = pl.pallas_call(
        lambda *refs: transform_kernel(
            *refs, group=group, lat_half=lat_half, lat_pad=lat_pad, bands=bands, mems=mems,
            members=members, rows=rows, pairs=pairs, lon_width=lon_width,
            first_steps=first_steps,
        ),
        out_shape=(
            pltpu.VMEM((stack, rows, longitudes), BF16),
            pltpu.VMEM((share, stack), F32),
        ),
        grid=(pair_steps + longitudes // 2 // lon_width,),
        in_specs=[
            pl.BlockSpec(memory_space=pltpu.SMEM),
            pl.BlockSpec(memory_space=pltpu.SMEM),
            pl.BlockSpec(memory_space=pltpu.HBM),
            pl.BlockSpec(memory_space=pltpu.HBM),
            pl.BlockSpec(memory_space=pltpu.HBM),
            pl.BlockSpec(memory_space=pltpu.HBM),
        ],
        out_specs=(fixed(stack, rows, longitudes), fixed(share, stack)),
        scratch_shapes=[
            pltpu.VMEM((pair_steps, stack, re_im, group * pair_len), BF16),
            pltpu.VMEM((pair_steps, lat_half, group * pair_len), BF16),
            pltpu.VMEM((2 * rows * bands, 4 * lat_pad), BF16),
            pltpu.VMEM((pairs, bands, width), F32),
            pltpu.VMEM(first_shape, BF16),
            pltpu.VMEM(first_shape, BF16),
            pltpu.VMEM(last_shape, BF16),
            pltpu.VMEM(last_shape, BF16),
            pltpu.VMEM((2, 2 * rows * stack, HALF), BF16),
            pltpu.VMEM((modes, stack), F32),
            pltpu.VMEM((bands, *folded), F32),
            pltpu.VMEM((bands, *folded), F32),
            pltpu.VMEM((mems, *folded), F32),
            pltpu.VMEM(table.shape, BF16),
            pltpu.VMEM(eof_basis.shape, BF16),
            dma((bands,)),
            dma((bands,)),
            dma((bands,)),
            dma((bands,)),
            dma((bands,)),
            dma((bands,)),
            dma((mems,)),
            dma((mems,)),
            dma((2,)),
            dma((2, pair_steps)),
        ],
        compiler_params=pltpu.CompilerParams(
            vmem_limit_bytes=VMEM_LIMIT, collective_id=0, has_side_effects=True
        ),
        name="transform",
    )(
        pair_waves,
        band_lengths,
        spectra.reshape(stack, re_im, slot_count),
        legendre,
        jnp.asarray(table),
        eof_basis,
    )
    grid_fields = grid.reshape(members, fields, levels, rows, longitudes)
    return (grid_fields, anomaly.T.reshape(members, fields, levels, share))


def solution(mesh):
    return jax.shard_map(
        shards,
        mesh=mesh,
        in_specs=(
            P("mem", None, None, None, "band"),
            P(None, "band"),
            P("band"),
            P(),
            P("band", None, None),
        ),
        out_specs=(P("mem", None, None, "band", None), P("mem", None, None, "band")),
        check_vma=False,
    )
```

```python
import math

import jax
import jax.numpy as jnp
import ml_dtypes
import numpy as np
from jax import lax
from jax.experimental import pallas as pl
from jax.experimental.pallas import tpu as pltpu
from jax.sharding import PartitionSpec as P

WAVE_COUNT = 1280
BLK = 128
HALF = WAVE_COUNT // 2
F32 = jnp.float32
BF16 = jnp.bfloat16
VMEM_LIMIT = 58 * 1024 * 1024


def iota(shape, axis):
    return lax.broadcasted_iota(jnp.int32, shape, axis)


def round_up(number, multiple):
    return -(-number // multiple) * multiple


def group_of(count, most):
    return max(size for size in range(1, most + 1) if count % size == 0)


def row_of(scalars, count, width):
    lane = iota((1, width), 1)
    values = jnp.zeros((1, width), jnp.int32)
    for index in range(count):
        values = jnp.where(lane == index, scalars[index], values)
    return values


def transform_kernel(
    waves_smem, lengths_smem, spectra_hbm, legendre_hbm, table_hbm, eof_hbm, grid_ref, anomaly_ref,
    spectra_ref, legendre_ref, select_ref, total_ref, first_out_ref, first_in_ref, last_out_ref, last_in_ref,
    waves_in_ref, projection_ref,
    shares_ref, shares_in_ref, members_ref, table_ref, eof_ref,
    first_send_sem, first_recv_sem, last_send_sem, last_recv_sem, share_send_sem, share_recv_sem,
    mem_send_sem, mem_recv_sem, local_sem, input_sem,
    *, group, lat_half, lat_pad, bands, mems, members, rows, pairs, lon_width, first_steps,
):
    step = pl.program_id(0)
    steps = pl.num_programs(0)
    pair_steps = pairs // group
    span_len = legendre_ref.shape[2]
    pair_len = span_len // group
    fields = spectra_ref.shape[1]
    first_pairs = first_steps * group
    columns = 2 * fields
    width = 2 * rows * columns
    quarter = rows * fields
    me = lax.axis_index("band")
    my_mem = lax.axis_index("mem")
    table_copy = pltpu.make_async_copy(table_hbm, table_ref, local_sem.at[0])
    eof_copy = pltpu.make_async_copy(eof_hbm, eof_ref, local_sem.at[1])

    def input_copies(index):
        span = pl.ds(pl.multiple_of(index * span_len, BLK), span_len)
        return (
            pltpu.make_async_copy(
                spectra_hbm.at[:, :, span], spectra_ref.at[index], input_sem.at[0, index]
            ),
            pltpu.make_async_copy(
                legendre_hbm.at[:, span], legendre_ref.at[index], input_sem.at[1, index]
            ),
        )

    def band_copies(source, landing, sends, receives):
        copies = []
        for hop in range(1, bands):
            peer = lax.rem(me + hop, bands)
            copies.append(
                pltpu.make_async_remote_copy(
                    src_ref=source.at[peer],
                    dst_ref=landing.at[me],
                    send_sem=sends.at[hop],
                    recv_sem=receives.at[hop],
                    device_id=(peer, my_mem),
                    device_id_type=pl.DeviceIdType.MESH,
                )
            )
        return copies

    @pl.when(step == 0)
    def _():
        for index in range(pair_steps):
            for copy in input_copies(index):
                copy.start()
        barrier = pltpu.get_barrier_semaphore()
        for hop in range(1, bands):
            pl.semaphore_signal(
                barrier, inc=1, device_id=(lax.rem(me + hop, bands), my_mem),
                device_id_type=pl.DeviceIdType.MESH,
            )
        for hop in range(1, mems):
            pl.semaphore_signal(
                barrier, inc=1, device_id=(me, lax.rem(my_mem + hop, mems)),
                device_id_type=pl.DeviceIdType.MESH,
            )
        table_copy.start()
        eof_copy.start()
        shape = (2 * rows * bands, 4 * lat_pad)
        slot = iota((2 * rows * bands, bands), 0)
        band = slot % bands
        lane = iota((2 * rows * bands, bands), 1)
        lengths = row_of(lengths_smem, bands, bands)
        start = jnp.sum(jnp.where(lane < band, lengths, 0).astype(F32), axis=1, keepdims=True)
        own = jnp.sum(jnp.where(lane == band, lengths, 0).astype(F32), axis=1, keepdims=True)
        slot = iota(shape, 0)
        row = slot // bands % rows
        place = iota(shape, 1)
        lat = jnp.broadcast_to(start, shape).astype(jnp.int32) + row
        keep = row < jnp.broadcast_to(own, shape).astype(jnp.int32)
        wanted = jnp.where(lat < lat_half, lat, lat_pad + 2 * lat_half - 1 - lat)
        wanted = wanted + slot // (bands * rows) * (2 * lat_pad)
        select_ref[...] = jnp.where(keep & (place == wanted), 1.0, 0.0).astype(BF16)

    @pl.when(step < pair_steps)
    def _():
        for copy in input_copies(step):
            copy.wait()
        position = iota((lat_pad, pair_len), 1)
        sign = jnp.where(position % 2 == 0, 1.0, -1.0)
        lane_in = iota((width, width), 0)
        lane_out = iota((width, width), 1)
        block, rest = lane_in // columns, lane_in % columns
        target = ((block // rows * 2 + rest % 2) * rows + block % rows) * fields + rest // 2
        reorder = (lane_out == target).astype(BF16)
        sums = []
        for index in range(group):
            span = slice(index * pair_len, (index + 1) * pair_len)
            lower = waves_smem[step * group + index]
            high_start = WAVE_COUNT - lower // BLK * BLK
            low = position < WAVE_COUNT - lower
            high = (position >= high_start) & (position < high_start + lower + 1)
            north = legendre_ref[step, :, span].astype(F32)
            north = jnp.concatenate(
                [north, jnp.zeros((lat_pad - lat_half, pair_len), F32)], axis=0
            )
            low_part = jnp.where(low, north, 0.0)
            high_part = jnp.where(high, north, 0.0)
            weights = jnp.concatenate(
                [low_part, low_part * sign, high_part, high_part * sign], axis=0
            ).astype(BF16)
            coeffs = spectra_ref[step, :, :, span].reshape(columns, pair_len)
            sums.append(
                lax.dot_general(coeffs, weights, (((1,), (1,)), ((), ())), preferred_element_type=F32)
            )
        fourier = jnp.concatenate(sums, axis=0).astype(BF16)
        picked = lax.dot_general(
            select_ref[...], fourier, (((1,), (1,)), ((), ())), preferred_element_type=F32
        )
        wide = jnp.concatenate(
            [
                jnp.concatenate(
                    [
                        picked[i * bands : (i + 1) * bands, index * columns : (index + 1) * columns]
                        for i in range(2 * rows)
                    ],
                    axis=1,
                )
                for index in range(group)
            ],
            axis=0,
        ).astype(BF16)
        wide = jnp.dot(wide, reorder, preferred_element_type=F32).reshape(group, bands, width)
        total_ref[pl.ds(step * group, group)] = wide

    first_copies = band_copies(first_out_ref, first_in_ref, first_send_sem, first_recv_sem)

    @pl.when(step == first_steps - 1)
    def _():
        pad = first_out_ref.shape[1] - first_pairs
        waves = row_of(waves_smem, pairs, width)
        kind = iota((pad, width), 0)
        extra = jnp.where(
            kind == 0, (waves // BLK).astype(F32), jnp.where(kind == 1, (waves % BLK).astype(F32), 0.0)
        )
        total = jnp.swapaxes(total_ref[:first_pairs], 0, 1)
        extra = jnp.broadcast_to(extra[None], (bands, pad, width))
        first_out_ref[...] = jnp.concatenate([total, extra], axis=1).astype(BF16)
        pl.semaphore_wait(pltpu.get_barrier_semaphore(), bands + mems - 2)
        for copy in first_copies:
            copy.start()
        first_in_ref[me] = first_out_ref[me]

    @pl.when(step == pair_steps - 1)
    def _():
        total = jnp.swapaxes(total_ref[first_pairs:], 0, 1)
        pad = last_out_ref.shape[1] - (pairs - first_pairs)
        if pad:
            total = jnp.concatenate([total, jnp.zeros((bands, pad, width), F32)], axis=1)
        last_out_ref[...] = total.astype(BF16)
        last_copies = band_copies(last_out_ref, last_in_ref, last_send_sem, last_recv_sem)
        for copy in last_copies:
            copy.start()
        last_in_ref[me] = last_out_ref[me]
        projection_ref[...] = jnp.zeros_like(projection_ref)
        for copy in first_copies:
            copy.wait()
        arrived = first_in_ref[...]
        coded = arrived[:, first_pairs:].astype(F32)
        high = jnp.sum(jnp.where(iota(coded.shape, 1) == 0, coded, 0.0), axis=1)
        low = jnp.sum(jnp.where(iota(coded.shape, 1) == 1, coded, 0.0), axis=1)
        waves = high * BLK + low

        def match_of(offset, held, taken):
            spread = jnp.broadcast_to(waves[:, None, :], (bands, taken, width))
            slot = iota(spread.shape, 1)
            lane = iota(spread.shape, 2)
            own = jnp.sum(jnp.where(slot + offset == lane, spread, 0.0), axis=2, keepdims=True)
            own = jnp.where(iota(own.shape, 1) < held, own, -1.0).reshape(bands * taken, 1)
            place = iota((bands * taken, HALF), 1)
            order = jnp.where(place < HALF // 2, 2 * place, 2 * place - (HALF - 1)).astype(F32)
            return jnp.where(own == order, 1.0, 0.0).astype(BF16)

        def placed(values, match):
            return lax.dot_general(
                values.reshape(match.shape[0], width), match, (((0,), (0,)), ((), ())),
                preferred_element_type=F32,
            )

        first_match = match_of(0, first_pairs, first_in_ref.shape[1])
        last_match = match_of(first_pairs, pairs - first_pairs, last_in_ref.shape[1])
        ordered = placed(arrived, first_match)
        for copy in last_copies:
            copy.wait()
        ordered += placed(last_in_ref[...], last_match)
        first_half = iota((2 * quarter, HALF), 1) < HALF // 2
        low_order, high_order = ordered[: 2 * quarter], ordered[2 * quarter :]
        waves_in_ref[0] = jnp.where(first_half, low_order, high_order).astype(BF16)
        waves_in_ref[1] = jnp.where(first_half, high_order, low_order).astype(BF16)
        table_copy.wait()
        eof_copy.wait()

    @pl.when(step >= pair_steps)
    def _():
        place = step - pair_steps
        span = pl.ds(pl.multiple_of(place * lon_width, lon_width), lon_width)
        even, odd = (
            jnp.dot(
                waves_in_ref[parity, :quarter], table_ref[parity, 0, :, span],
                preferred_element_type=F32,
            )
            + jnp.dot(
                waves_in_ref[parity, quarter:], table_ref[parity, 1, :, span],
                preferred_element_type=F32,
            )
            for parity in range(2)
        )
        total = projection_ref[...]
        for base, value in ((0, even + odd), (steps - pair_steps, even - odd)):
            parts = [value[row * fields : (row + 1) * fields] for row in range(rows)]
            span = pl.ds(pl.multiple_of((base + place) * lon_width, lon_width), lon_width)
            grid_ref[:, :, span] = jnp.stack(parts, axis=1).astype(BF16)
            for row in range(rows):
                total += lax.dot_general(
                    eof_ref[row, span, :], parts[row].astype(BF16), (((0,), (1,)), ((), ())),
                    preferred_element_type=F32,
                )
        projection_ref[...] = total

    @pl.when(step == steps - 1)
    def _():
        fold = shares_ref.shape[2] // fields
        high = shares_ref.shape[1]
        shares = projection_ref[...].reshape(bands, fold * high, fields)
        shares_ref[...] = jnp.concatenate(
            [shares[:, i * high : (i + 1) * high] for i in range(fold)], axis=2
        )
        copies = band_copies(shares_ref, shares_in_ref, share_send_sem, share_recv_sem)
        for copy in copies:
            copy.start()
        shares_in_ref[me] = shares_ref[me]
        for copy in copies:
            copy.wait()
        own = jnp.sum(shares_in_ref[...], axis=0)
        members_ref[my_mem] = own
        copies = []
        for hop in range(1, mems):
            peer = lax.rem(my_mem + hop, mems)
            copies.append(
                pltpu.make_async_remote_copy(
                    src_ref=members_ref.at[my_mem],
                    dst_ref=members_ref.at[my_mem],
                    send_sem=mem_send_sem.at[hop],
                    recv_sem=mem_recv_sem.at[hop],
                    device_id=(me, peer),
                    device_id_type=pl.DeviceIdType.MESH,
                )
            )
        for copy in copies:
            copy.start()
        for copy in copies:
            copy.wait()

        def unfolded(value):
            return jnp.concatenate(
                [value[:, i * fields : (i + 1) * fields] for i in range(fold)], axis=0
            )

        total = unfolded(jnp.sum(members_ref[...], axis=0))
        stack = fields // members
        mean = sum(total[:, i * stack : (i + 1) * stack] for i in range(members)) / (members * mems)
        anomaly_ref[...] = unfolded(own) - jnp.concatenate([mean] * members, axis=1)


def wave_tables(longitudes):
    place = np.arange(HALF)
    lower = np.where(place < HALF // 2, 2 * place, 2 * place - (HALF - 1))
    upper = WAVE_COUNT - 1 - lower
    even = np.where(lower % 2 == 0, lower, upper)
    orders = np.stack([even, WAVE_COUNT - 1 - even])
    phase = orders[..., None] * np.arange(longitudes // 2) % longitudes
    angle = phase * (2.0 * math.pi / longitudes)
    weight = np.where(orders == 0, 1.0, 2.0)[..., None]
    table = np.stack([weight * np.cos(angle), -weight * np.sin(angle)], axis=1)
    return table.astype(np.float32).astype(ml_dtypes.bfloat16)


def shards(spectra, legendre, pair_waves, band_lengths, eof_basis):
    members, fields, levels, re_im, slot_count = spectra.shape
    lat_half = legendre.shape[0]
    pairs = pair_waves.shape[0]
    pair_len = slot_count // pairs
    stack = members * fields * levels
    bands = lax.axis_size("band")
    rows, longitudes, modes = eof_basis.shape
    width = 2 * rows * stack * re_im
    group = group_of(pairs, 8)
    lat_pad = round_up(lat_half, 16)
    mems = lax.axis_size("mem")

    def fixed(*shape):
        return pl.BlockSpec(shape, lambda *_: (0,) * len(shape))

    lon_width = math.gcd(longitudes // 2, 640)
    pair_steps = pairs // group
    first_steps = (pair_steps + 1) // 2
    first_pairs = first_steps * group
    first_shape = (bands, round_up(first_pairs + 2, 16), width)
    last_shape = (bands, round_up(pairs - first_pairs, 16), width)
    table = wave_tables(longitudes)
    share = modes // bands
    fold = max(1, share // 8)
    folded = (share // fold, fold * stack)
    dma = pltpu.SemaphoreType.DMA
    grid, anomaly = pl.pallas_call(
        lambda *refs: transform_kernel(
            *refs, group=group, lat_half=lat_half, lat_pad=lat_pad, bands=bands, mems=mems,
            members=members, rows=rows, pairs=pairs, lon_width=lon_width,
            first_steps=first_steps,
        ),
        out_shape=(
            pltpu.VMEM((stack, rows, longitudes), BF16),
            pltpu.VMEM((share, stack), F32),
        ),
        grid=(pair_steps + longitudes // 2 // lon_width,),
        in_specs=[
            pl.BlockSpec(memory_space=pltpu.SMEM),
            pl.BlockSpec(memory_space=pltpu.SMEM),
            pl.BlockSpec(memory_space=pltpu.HBM),
            pl.BlockSpec(memory_space=pltpu.HBM),
            pl.BlockSpec(memory_space=pltpu.HBM),
            pl.BlockSpec(memory_space=pltpu.HBM),
        ],
        out_specs=(fixed(stack, rows, longitudes), fixed(share, stack)),
        scratch_shapes=[
            pltpu.VMEM((pair_steps, stack, re_im, group * pair_len), BF16),
            pltpu.VMEM((pair_steps, lat_half, group * pair_len), BF16),
            pltpu.VMEM((2 * rows * bands, 4 * lat_pad), BF16),
            pltpu.VMEM((pairs, bands, width), F32),
            pltpu.VMEM(first_shape, BF16),
            pltpu.VMEM(first_shape, BF16),
            pltpu.VMEM(last_shape, BF16),
            pltpu.VMEM(last_shape, BF16),
            pltpu.VMEM((2, 2 * rows * stack, HALF), BF16),
            pltpu.VMEM((modes, stack), F32),
            pltpu.VMEM((bands, *folded), F32),
            pltpu.VMEM((bands, *folded), F32),
            pltpu.VMEM((mems, *folded), F32),
            pltpu.VMEM(table.shape, BF16),
            pltpu.VMEM(eof_basis.shape, BF16),
            dma((bands,)),
            dma((bands,)),
            dma((bands,)),
            dma((bands,)),
            dma((bands,)),
            dma((bands,)),
            dma((mems,)),
            dma((mems,)),
            dma((2,)),
            dma((2, pair_steps)),
        ],
        compiler_params=pltpu.CompilerParams(
            vmem_limit_bytes=VMEM_LIMIT, collective_id=0, has_side_effects=True
        ),
        name="transform",
    )(
        pair_waves,
        band_lengths,
        spectra.reshape(stack, re_im, slot_count),
        legendre,
        jnp.asarray(table),
        eof_basis,
    )
    grid_fields = grid.reshape(members, fields, levels, rows, longitudes)
    return (grid_fields, anomaly.T.reshape(members, fields, levels, share))


def solution(mesh):
    return jax.shard_map(
        shards,
        mesh=mesh,
        in_specs=(
            P("mem", None, None, None, "band"),
            P(None, "band"),
            P("band"),
            P(),
            P("band", None, None),
        ),
        out_specs=(P("mem", None, None, "band", None), P("mem", None, None, "band")),
        check_vma=False,
    )
```
